32 devices in a mesh: rep: 16 (over z, y, x), shard: 2 (over core).
Axes of the slice: x: 2, y: 2, z: 4, core: 2. Of those that a mesh axis runs over, the one named last changes fastest.
Arguments:
- tokens: bfloat16 [32, 1024, 640], P(('rep', 'shard')), may hold values from -6 to 6
- segments: int32 [32, 1024], P(('rep', 'shard')), may hold values from 0 to 3, never falling along the last dimension, each value on 1 to 512 neighbouring positions
- w_query: bfloat16 [640, 1024], P('shard'), may hold values from -0.25 to 0.25
- w_key: bfloat16 [640, 256], P('shard'), may hold values from -0.25 to 0.25
- w_value: bfloat16 [640, 256], P('shard'), may hold values from -0.25 to 0.25
- w_output: bfloat16 [1024, 640], P('shard'), may hold values from -0.375 to 0.375
- w_gate: bfloat16 [640, 2048], P('shard'), may hold values from -0.25 to 0.25
- w_up: bfloat16 [640, 2048], P('shard'), may hold values from -0.25 to 0.25
- w_down: bfloat16 [2048, 640], P('shard'), may hold values from -0.125 to 0.125
- gain_input: bfloat16 [640], P('shard'), may hold values from 0.099609375 to 1.8984375
- gain_query: bfloat16 [256], P('shard'), may hold values from 0.099609375 to 1.8984375
- gain_key: bfloat16 [256], P('shard'), may hold values from 0.099609375 to 1.8984375
- gain_attend: bfloat16 [640], P('shard'), may hold values from 0.099609375 to 1.8984375
- gain_ffn: bfloat16 [640], P('shard'), may hold values from 0.099609375 to 1.8984375
- gain_post: bfloat16 [640], P('shard'), may hold values from 0.099609375 to 1.8984375
- cotangent: bfloat16 [32, 1024, 640], P(('rep', 'shard')), may hold values from -6 to 6
Outputs:
- outputs: bfloat16 [32, 1024, 640], P(('rep', 'shard'))
- grad_tokens: bfloat16 [32, 1024, 640], P(('rep', 'shard'))
- grad_query: float32 [640, 1024], P('shard')
- grad_key: float32 [640, 256], P('shard')
- grad_value: float32 [640, 256], P('shard')
- grad_output: float32 [1024, 640], P('shard')
- grad_gate: float32 [640, 2048], P('shard')
- grad_up: float32 [640, 2048], P('shard')
- grad_down: float32 [2048, 640], P('shard')
- grad_gain_input: float32 [640], P('shard')
- grad_gain_query: float32 [256], P('shard')
- grad_gain_key: float32 [256], P('shard')
- grad_gain_attend: float32 [640], P('shard')
- grad_gain_ffn: float32 [640], P('shard')
- grad_gain_post: float32 [640], P('shard')
The draws below stay inside these ranges and needn't reach their ends.
Inputs may be any that keep to these rules, and one draw needn't show every extreme that they name: `segments`: within each sequence segment numbers never fall; each document has 1 to 512 tokens, and one has exactly 512.
All inputs are finite; a program needn't handle non-finite values.
Results may differ from the reference program's by a relative error of at most 0.025.
Values may be sent and summed in bfloat16 or wider, within the bound.
A program may use at most 192 MiB of HBM per device.

```python
import math
import jax
import jax.numpy as jnp
import numpy as np
from jax import lax

D = 640
HEADS = 4
HD = 256
FF = 2048
LEN = 1024
DOCS = 4
DOC_MOST = 512
SEQS = 32


def block_levels(rng, shape, split, smallest, high):
    level, own = 1.0, jax.random.fold_in(rng, 6)
    for dim, shards_of in split:
        draws = jnp.exp(jax.random.uniform(jax.random.fold_in(own, dim), (shards_of,), jnp.float32, smallest / len(split), high / len(split)))
        level = level * jnp.repeat(draws, shape[dim] // shards_of).reshape([-1 if axis == dim else 1 for axis in range(len(shape))])
    return level


def length_profile(amount, total, limit, slope):
    loads = [(1 << 20) // math.isqrt(standing ** slope) + 1 for standing in range(2, amount + 1)]
    spare, counts = total - limit - (amount - 1), [1] * (amount - 1)
    while spare > 0:
        candidates = [i for i in range(amount - 1) if counts[i] < limit]
        pool, budget = sum([loads[i] for i in candidates]), spare
        for i in candidates:
            addition = min(limit - counts[i], max(1, budget * loads[i] // pool), spare)
            counts[i] = counts[i] + addition
            spare = spare - addition
    return np.array([limit] + counts)


def ragged(rng, amount, total, limit, lean):
    if amount == 2:
        one = jax.random.randint(rng, (), max(1, total - limit), min(limit, total - 1) + 1)
        return jnp.stack([one, total - one])
    lengths = jnp.asarray(length_profile(amount, total, limit, lean), jnp.int32)
    pairs = (amount - 1) // 2
    source_of, sink = lengths[1:1 + 2 * pairs:2], lengths[2:2 + 2 * pairs:2]
    slack = jnp.minimum(source_of - 1, limit - sink)
    moved = jax.random.randint(jax.random.fold_in(rng, 1), (pairs,), 0, 1 << 20) % (slack + 1)
    lengths = lengths.at[1:1 + 2 * pairs:2].set(source_of - moved).at[2:2 + 2 * pairs:2].set(sink + moved)
    return lengths[jax.random.permutation(jax.random.fold_in(rng, 2), amount)]


def scatter_about(stream_key, shape, scale, bound, split=(), kind=jnp.bfloat16):
    values = scale * jax.random.normal(stream_key, shape, jnp.float32)
    if split:
        values = values * block_levels(stream_key, shape, split, -0.22, 0.18)
    return jnp.clip(values, -bound, bound).astype(kind)


def setup_inputs(seed: int = 0) -> dict:
    key_list = jax.random.split(jax.random.key(seed), 17)
    return {
        "tokens": scatter_about(key_list[0], (SEQS, LEN, D), 1.0, 6.0, ((0, 32),)),
        "segments": jax.vmap(lambda own: jnp.searchsorted(jnp.cumsum(ragged(own, DOCS, LEN, DOC_MOST, 1)), jnp.arange(LEN), side="right"))(jax.random.split(key_list[1], SEQS)).reshape((SEQS, LEN)).astype(jnp.int32),
        "w_query": scatter_about(key_list[2], (D, HEADS * HD), D ** -0.5, 0.25, ((0, 2),)),
        "w_key": scatter_about(key_list[3], (D, HD), D ** -0.5, 0.25, ((0, 2),)),
        "w_value": scatter_about(key_list[4], (D, HD), D ** -0.5, 0.25, ((0, 2),)),
        "w_output": scatter_about(key_list[5], (HEADS * HD, D), HD ** -0.5, 0.375, ((0, 2),)),
        "w_gate": scatter_about(key_list[6], (D, FF), D ** -0.5, 0.25, ((0, 2),)),
        "w_up": scatter_about(key_list[7], (D, FF), D ** -0.5, 0.25, ((0, 2),)),
        "w_down": scatter_about(key_list[8], (FF, D), FF ** -0.5, 0.125, ((0, 2),)),
        "gain_input": jnp.clip(1.0 + 0.18 * jax.random.normal(key_list[9], (D,), jnp.float32), 0.099609375, 1.8984375).astype(jnp.bfloat16),
        "gain_query": jnp.clip(1.0 + 0.18 * jax.random.normal(key_list[10], (HD,), jnp.float32), 0.099609375, 1.8984375).astype(jnp.bfloat16),
        "gain_key": jnp.clip(1.0 + 0.18 * jax.random.normal(key_list[11], (HD,), jnp.float32), 0.099609375, 1.8984375).astype(jnp.bfloat16),
        "gain_attend": jnp.clip(1.0 + 0.18 * jax.random.normal(key_list[12], (D,), jnp.float32), 0.099609375, 1.8984375).astype(jnp.bfloat16),
        "gain_ffn": jnp.clip(1.0 + 0.18 * jax.random.normal(key_list[13], (D,), jnp.float32), 0.099609375, 1.8984375).astype(jnp.bfloat16),
        "gain_post": jnp.clip(1.0 + 0.18 * jax.random.normal(key_list[14], (D,), jnp.float32), 0.099609375, 1.8984375).astype(jnp.bfloat16),
        "cotangent": scatter_about(key_list[15], (SEQS, LEN, D), 1.0, 6.0, ((0, 32),)),
    }


EPS = 1e-06
THETA = 1000000.0

@jax.custom_vjp
def low(v):
    return lax.optimization_barrier(v.astype(jnp.bfloat16)).astype(jnp.float32)

@jax.custom_vjp
def low_back(v):
    return v

def low_keep(v):
    return (low(v), None)

def low_pass(kept, grad):
    return (grad,)

def back_keep(v):
    return (v, None)

def back_low(kept, grad):
    return (low(grad),)
low.defvjp(low_keep, low_pass)
low_back.defvjp(back_keep, back_low)

def matmul(left, right):
    return jnp.dot(left, right, precision=lax.Precision.HIGHEST, preferred_element_type=jnp.float32)

def norm_rows(values, gain):
    return values * lax.rsqrt(lax.optimization_barrier(jnp.mean(values * values, axis=-1, keepdims=True)) + EPS) * gain

def rotary(values, cosine, sine_part):
    halfway = values.shape[-1] // 2
    front = values[..., :halfway]
    behind = values[..., halfway:]
    return jnp.concatenate([front * cosine - behind * sine_part, behind * cosine + front * sine_part], axis=-1)

def rotary_tables(segment, width):
    length = segment.shape[0]
    indices = jnp.arange(length, dtype=jnp.int32)
    change = jnp.concatenate([jnp.ones((1,), dtype=bool), segment[1:] != segment[:-1]])
    starts = lax.cummax(jnp.where(change, indices, 0), axis=0)
    position = (indices - starts).astype(jnp.float32)
    halfway = width // 2
    frequency = THETA ** (-(2.0 * jnp.arange(halfway, dtype=jnp.float32)) / (2.0 * halfway))
    turned = position[:, None] * frequency[None, :]
    return (jnp.cos(turned), jnp.sin(turned))

def layer(inputs, segment, weights):
    w_query, w_key, w_value, w_output, w_gate, w_up, w_down, gain_input, gain_query, gain_key, gain_attend, gain_ffn, gain_post = weights
    length = inputs.shape[0]
    cosine, sine_part = rotary_tables(segment, HD)
    normed = low(norm_rows(inputs, gain_input))
    queries = low_back(matmul(normed, w_query)).reshape(length, HEADS, HD)
    key_raw = low_back(matmul(normed, w_key))
    values = low(low_back(matmul(normed, w_value)))
    queries = low(rotary(norm_rows(queries, gain_query), cosine[:, None, :], sine_part[:, None, :]) * HD ** (-0.5))
    keys_rot = low(rotary(norm_rows(key_raw, gain_key), cosine, sine_part))
    scores = low_back(jnp.einsum('lhd,md->hlm', queries, keys_rot, precision=lax.Precision.HIGHEST))
    indices = jnp.arange(length, dtype=jnp.int32)
    allowed = (segment[:, None] == segment[None, :]) & (indices[:, None] >= indices[None, :])
    scores = jnp.where(allowed[None], scores, -1e+30)
    largest = lax.optimization_barrier(jnp.max(scores, axis=-1, keepdims=True))
    expd = jnp.exp(scores - largest)
    probabilities = expd / lax.optimization_barrier(jnp.sum(expd, axis=-1, keepdims=True))
    attended = jnp.einsum('hlm,md->lhd', low(probabilities), values, precision=lax.Precision.HIGHEST)
    attended = low(low_back(attended)).reshape(length, HEADS * HD)
    branch = low_back(matmul(attended, w_output))
    middle = inputs + norm_rows(branch, gain_attend)
    normed_two = low(norm_rows(middle, gain_ffn))
    gate_out = low_back(matmul(normed_two, w_gate))
    upward = low_back(matmul(normed_two, w_up))
    hidden = low(jax.nn.gelu(gate_out, approximate=True) * upward)
    branch_two = low_back(matmul(hidden, w_down))
    return middle + norm_rows(branch_two, gain_post)

def reference(tokens, segments, w_query, w_key, w_value, w_output, w_gate, w_up, w_down, gain_input, gain_query, gain_key, gain_attend, gain_ffn, gain_post, cotangent):
    weights = tuple((tensor.astype(jnp.float32) for tensor in (w_query, w_key, w_value, w_output, w_gate, w_up, w_down, gain_input, gain_query, gain_key, gain_attend, gain_ffn, gain_post)))
    zeroed = jax.tree.map(jnp.zeros_like, weights)

    def per_sequence(totals, slices):
        inputs, segment, incoming = slices
        result, pullback = jax.vjp(lambda source, params: layer(source, segment, params), inputs.astype(jnp.float32), weights)
        grad_in, grad_weights = pullback(incoming.astype(jnp.float32))
        totals = jax.tree.map(jnp.add, totals, grad_weights)
        return (totals, (result.astype(jnp.bfloat16), grad_in.astype(jnp.bfloat16)))
    totals, (outputs, grad_tokens) = lax.scan(per_sequence, zeroed, (tokens, segments, cotangent))
    return (outputs, grad_tokens, totals[0], totals[1], totals[2], totals[3], totals[4], totals[5], totals[6], totals[7], totals[8], totals[9], totals[10], totals[11], totals[12])
```

```python
import functools

import jax
import jax.numpy as jnp
from jax import lax
from jax.sharding import PartitionSpec as P

EPS = 1e-06
THETA = 1000000.0
BLOCK = 256
DOC_MOST = 512


def norm_rows(values, gain):
    return values * lax.rsqrt(jnp.mean(values * values, axis=-1, keepdims=True) + EPS) * gain


def rotary(values, cosine, sine_part):
    halfway = values.shape[-1] // 2
    front = values[..., :halfway]
    behind = values[..., halfway:]
    return jnp.concatenate(
        [front * cosine - behind * sine_part, behind * cosine + front * sine_part], axis=-1
    )


def rotary_tables(segment, width):
    length = segment.shape[0]
    indices = jnp.arange(length, dtype=jnp.int32)
    change = jnp.concatenate([jnp.ones((1,), dtype=bool), segment[1:] != segment[:-1]])
    starts = lax.cummax(jnp.where(change, indices, 0), axis=0)
    position = (indices - starts).astype(jnp.float32)
    halfway = width // 2
    frequency = THETA ** (-(2.0 * jnp.arange(halfway, dtype=jnp.float32)) / (2.0 * halfway))
    turned = position[:, None] * frequency[None, :]
    return (jnp.cos(turned), jnp.sin(turned))


def glu_part(gate_out, upward):
    return jax.nn.gelu(gate_out, approximate=True) * upward


def block_mask(segment, start, low, high):
    rows_idx = jnp.arange(start, high, dtype=jnp.int32)
    cols_idx = jnp.arange(low, high, dtype=jnp.int32)
    same_doc = segment[start:high][:, None] == segment[low:high][None, :]
    return same_doc & (rows_idx[:, None] >= cols_idx[None, :])


def forward(inputs, segment, mats):
    (
        w_query,
        w_key,
        w_value,
        w_output,
        w_gate,
        w_up,
        w_down,
        gain_input,
        gain_query,
        gain_key,
        gain_attend,
        gain_ffn,
        gain_post,
    ) = mats
    length = inputs.shape[0]
    width = w_key.shape[1]
    heads = w_query.shape[1] // width
    block = min(BLOCK, length)
    cosine, sine_part = rotary_tables(segment, width)
    normed = norm_rows(inputs, gain_input.astype(jnp.float32)).astype(jnp.bfloat16)
    query_raw = jnp.dot(normed, w_query, preferred_element_type=jnp.float32).reshape(
        length, heads, width
    )
    key_raw = jnp.dot(normed, w_key, preferred_element_type=jnp.float32)
    values = jnp.dot(normed, w_value, preferred_element_type=jnp.float32).astype(jnp.bfloat16)
    queries = (
        rotary(
            norm_rows(query_raw, gain_query.astype(jnp.float32)),
            cosine[:, None, :],
            sine_part[:, None, :],
        )
        * width ** (-0.5)
    ).astype(jnp.bfloat16)
    keys_rot = rotary(norm_rows(key_raw, gain_key.astype(jnp.float32)), cosine, sine_part).astype(
        jnp.bfloat16
    )
    pieces = []
    kept_probs = []
    for start in range(0, length, block):
        low = max(0, start - DOC_MOST)
        high = start + block
        scores = jnp.einsum(
            "lhd,md->hlm",
            queries[start:high],
            keys_rot[low:high],
            preferred_element_type=jnp.float32,
        )
        allowed = block_mask(segment, start, low, high)
        scores = jnp.where(allowed[None], scores, -1e30)
        largest = jnp.max(scores, axis=-1, keepdims=True)
        expd = jnp.exp(scores - largest)
        totals = jnp.sum(expd, axis=-1, keepdims=True)
        probabilities = (expd / totals).astype(jnp.bfloat16)
        kept_probs.append(probabilities)
        pieces.append(
            jnp.einsum(
                "hlm,md->lhd", probabilities, values[low:high], preferred_element_type=jnp.float32
            )
        )
    attended = jnp.concatenate(pieces, axis=0).astype(jnp.bfloat16).reshape(length, heads * width)
    branch = jnp.dot(attended, w_output, preferred_element_type=jnp.float32)
    middle = inputs + norm_rows(branch, gain_attend.astype(jnp.float32))
    normed_two = norm_rows(middle, gain_ffn.astype(jnp.float32)).astype(jnp.bfloat16)
    gate_out = jnp.dot(normed_two, w_gate, preferred_element_type=jnp.float32)
    upward = jnp.dot(normed_two, w_up, preferred_element_type=jnp.float32)
    hidden = glu_part(gate_out, upward).astype(jnp.bfloat16)
    branch_two = jnp.dot(hidden, w_down, preferred_element_type=jnp.float32)
    result = middle + norm_rows(branch_two, gain_post.astype(jnp.float32))
    kept = (
        inputs,
        segment,
        cosine,
        sine_part,
        normed,
        query_raw,
        key_raw,
        values,
        queries,
        keys_rot,
        kept_probs,
        attended,
        branch,
        middle,
        normed_two,
        gate_out,
        upward,
        hidden,
        branch_two,
    )
    return (result, kept)


def backward_ffn(kept, incoming, mats):
    (
        w_query,
        w_key,
        w_value,
        w_output,
        w_gate,
        w_up,
        w_down,
        gain_input,
        gain_query,
        gain_key,
        gain_attend,
        gain_ffn,
        gain_post,
    ) = mats
    (
        inputs,
        segment,
        cosine,
        sine_part,
        normed,
        query_raw,
        key_raw,
        values,
        queries,
        keys_rot,
        kept_probs,
        attended,
        branch,
        middle,
        normed_two,
        gate_out,
        upward,
        hidden,
        branch_two,
    ) = kept
    grad_out = incoming.astype(jnp.float32)
    unused, pull_post = jax.vjp(norm_rows, branch_two, gain_post.astype(jnp.float32))
    d_branch_two, g_post = pull_post(grad_out)
    d_branch_two = d_branch_two.astype(jnp.bfloat16)
    gw_down = jnp.einsum("lf,ld->fd", hidden, d_branch_two, preferred_element_type=jnp.float32)
    d_hidden = jnp.einsum("ld,fd->lf", d_branch_two, w_down, preferred_element_type=jnp.float32)
    unused, pull_glu = jax.vjp(glu_part, gate_out, upward)
    d_gate, d_up = pull_glu(d_hidden)
    d_gate = d_gate.astype(jnp.bfloat16)
    d_up = d_up.astype(jnp.bfloat16)
    gw_gate = jnp.einsum("ld,lf->df", normed_two, d_gate, preferred_element_type=jnp.float32)
    gw_up = jnp.einsum("ld,lf->df", normed_two, d_up, preferred_element_type=jnp.float32)
    d_normed_two = jnp.einsum(
        "lf,df->ld", d_gate, w_gate, preferred_element_type=jnp.float32
    ) + jnp.einsum("lf,df->ld", d_up, w_up, preferred_element_type=jnp.float32)
    unused, pull_ffn = jax.vjp(norm_rows, middle, gain_ffn.astype(jnp.float32))
    d_mid_part, g_ffn = pull_ffn(d_normed_two)
    d_middle = grad_out + d_mid_part
    return (d_middle, (gw_gate, gw_up, gw_down, g_ffn, g_post))


def backward_attn(kept, d_middle, mats):
    (
        w_query,
        w_key,
        w_value,
        w_output,
        w_gate,
        w_up,
        w_down,
        gain_input,
        gain_query,
        gain_key,
        gain_attend,
        gain_ffn,
        gain_post,
    ) = mats
    (
        inputs,
        segment,
        cosine,
        sine_part,
        normed,
        query_raw,
        key_raw,
        values,
        queries,
        keys_rot,
        kept_probs,
        attended,
        branch,
        middle,
        normed_two,
        gate_out,
        upward,
        hidden,
        branch_two,
    ) = kept
    length = inputs.shape[0]
    width = w_key.shape[1]
    heads = w_query.shape[1] // width
    block = min(BLOCK, length)
    unused, pull_attend = jax.vjp(norm_rows, branch, gain_attend.astype(jnp.float32))
    d_branch, g_attend = pull_attend(d_middle)
    d_branch = d_branch.astype(jnp.bfloat16)
    gw_output = jnp.einsum("la,ld->ad", attended, d_branch, preferred_element_type=jnp.float32)
    d_attended = jnp.einsum("ld,ad->la", d_branch, w_output, preferred_element_type=jnp.float32)
    d_attended = d_attended.astype(jnp.bfloat16).reshape(length, heads, width)
    attended_heads = attended.reshape(length, heads, width)
    delta = jnp.sum(
        d_attended.astype(jnp.float32) * attended_heads.astype(jnp.float32), axis=-1
    ).T
    d_keys = [0.0] * (length // block)
    d_values = [0.0] * (length // block)
    d_query_parts = []
    for number, start in enumerate(range(0, length, block)):
        low = max(0, start - DOC_MOST)
        high = start + block
        rows_q = queries[start:high]
        rows_d = d_attended[start:high]
        probabilities = kept_probs[number]
        value_term = jnp.einsum(
            "hlm,lhd->md", probabilities, rows_d, preferred_element_type=jnp.float32
        )
        d_probs = jnp.einsum(
            "lhd,md->hlm", rows_d, values[low:high], preferred_element_type=jnp.float32
        )
        d_scores = probabilities.astype(jnp.float32) * (d_probs - delta[:, start:high, None])
        d_scores = d_scores.astype(jnp.bfloat16)
        d_query_parts.append(
            jnp.einsum(
                "hlm,md->lhd", d_scores, keys_rot[low:high], preferred_element_type=jnp.float32
            )
        )
        key_term = jnp.einsum("hlm,lhd->md", d_scores, rows_q, preferred_element_type=jnp.float32)
        for part in range(low // block, high // block):
            rows = slice(part * block - low, part * block - low + block)
            d_keys[part] = d_keys[part] + key_term[rows]
            d_values[part] = d_values[part] + value_term[rows]
    d_queries = jnp.concatenate(d_query_parts, axis=0)
    d_keys = jnp.concatenate(d_keys, axis=0)
    d_values = jnp.concatenate(d_values, axis=0)

    def query_map(raw_query, gain_value):
        return rotary(
            norm_rows(raw_query, gain_value), cosine[:, None, :], sine_part[:, None, :]
        ) * width ** (-0.5)

    def key_map(raw_key, gain_value):
        return rotary(norm_rows(raw_key, gain_value), cosine, sine_part)

    unused, pull_query = jax.vjp(query_map, query_raw, gain_query.astype(jnp.float32))
    d_query_raw, g_query = pull_query(d_queries)
    d_query_raw = d_query_raw.astype(jnp.bfloat16).reshape(length, heads * width)
    unused, pull_key = jax.vjp(key_map, key_raw, gain_key.astype(jnp.float32))
    d_key_raw, g_key = pull_key(d_keys)
    d_key_raw = d_key_raw.astype(jnp.bfloat16)
    d_values = d_values.astype(jnp.bfloat16)
    gw_query = jnp.einsum("ld,lq->dq", normed, d_query_raw, preferred_element_type=jnp.float32)
    gw_key = jnp.einsum("ld,lq->dq", normed, d_key_raw, preferred_element_type=jnp.float32)
    gw_value = jnp.einsum("ld,lq->dq", normed, d_values, preferred_element_type=jnp.float32)
    d_normed = (
        jnp.einsum("lq,dq->ld", d_query_raw, w_query, preferred_element_type=jnp.float32)
        + jnp.einsum("lq,dq->ld", d_key_raw, w_key, preferred_element_type=jnp.float32)
        + jnp.einsum("lq,dq->ld", d_values, w_value, preferred_element_type=jnp.float32)
    )
    unused, pull_input = jax.vjp(norm_rows, inputs, gain_input.astype(jnp.float32))
    d_in_part, g_input = pull_input(d_normed)
    grad_inputs = d_middle + d_in_part
    return (grad_inputs, (gw_query, gw_key, gw_value, gw_output, g_input, g_query, g_key, g_attend))


def flip_bit(size, bit):
    return [(i, i ^ (1 << bit)) for i in range(size)]


def half_axis(shape):
    if shape[1] % 256 == 0:
        return 1
    if shape[0] % 2 == 0:
        return 0
    return 1


def halves(x, axis):
    half = x.shape[axis] // 2
    return (
        lax.slice_in_dim(x, 0, half, axis=axis),
        lax.slice_in_dim(x, half, 2 * half, axis=axis),
    )


def exchange_sum(x, name, size, bit, axis):
    upper = ((lax.axis_index(name) >> bit) & 1) == 1
    low, high = halves(x, axis)
    away = lax.ppermute(jnp.where(upper, low, high), name, flip_bit(size, bit))
    kept = jnp.where(upper, high, low)
    return (kept.astype(jnp.float32) + away.astype(jnp.float32)).astype(x.dtype)


def exchange_join(x, name, size, bit, axis):
    upper = ((lax.axis_index(name) >> bit) & 1) == 1
    other = lax.ppermute(x, name, flip_bit(size, bit))
    return jnp.concatenate(
        [jnp.where(upper, other, x), jnp.where(upper, x, other)], axis=axis
    )


def bit_count(size):
    count = size.bit_length() - 1
    assert size == 1 << count
    return count


def gather_rows(x, size):
    for bit in range(bit_count(size)):
        x = exchange_join(x, "shard", size, bit, 0)
    return x


def sum_all(parts, shards, replicas):
    parts = list(parts)
    for bit in reversed(range(bit_count(shards))):
        parts = [exchange_sum(x, "shard", shards, bit, 0) for x in parts]
    count = bit_count(replicas)
    orders = []
    for number in range(len(parts)):
        base = list(range(count - 1))
        turn = number % max(len(base), 1)
        orders.append(base[turn:] + base[:turn] + [count - 1])
    done = [[] for _ in parts]
    for step in range(count):
        for number in range(len(parts)):
            axis = half_axis(parts[number].shape)
            done[number].append((orders[number][step], axis))
            parts[number] = exchange_sum(
                parts[number], "rep", replicas, orders[number][step], axis
            )
    for step in reversed(range(count)):
        for number in range(len(parts)):
            bit, axis = done[number][step]
            parts[number] = exchange_join(parts[number], "rep", replicas, bit, axis)
    return parts


def per_device(
    shards,
    replicas,
    tokens,
    segments,
    w_query,
    w_key,
    w_value,
    w_output,
    w_gate,
    w_up,
    w_down,
    gain_input,
    gain_query,
    gain_key,
    gain_attend,
    gain_ffn,
    gain_post,
    cotangent,
):
    queries_wide = w_query.shape[1]
    width = w_key.shape[1]
    w_all = gather_rows(jnp.concatenate([w_query, w_key, w_value], axis=1), shards)
    owned_gains = (gain_input, gain_attend, gain_ffn, gain_post, gain_query, gain_key)
    packed = gather_rows(jnp.concatenate(owned_gains)[None], shards)
    gains = []
    place = 0
    for gain in owned_gains:
        gains.append(packed[:, place : place + gain.shape[0]].reshape(-1))
        place += gain.shape[0]
    mats = (
        w_all[:, :queries_wide],
        w_all[:, queries_wide : queries_wide + width],
        w_all[:, queries_wide + width :],
        lax.all_gather(w_output, "shard", axis=0, tiled=True),
        lax.all_gather(w_gate, "shard", axis=0, tiled=True),
        lax.all_gather(w_up, "shard", axis=0, tiled=True),
        lax.all_gather(w_down, "shard", axis=0, tiled=True),
        gains[0],
        gains[4],
        gains[5],
        gains[1],
        gains[2],
        gains[3],
    )
    result, kept = forward(tokens[0].astype(jnp.float32), segments[0], mats)
    d_middle, ffn_terms = backward_ffn(kept, cotangent[0], mats)
    ffn_parts = [t.astype(jnp.bfloat16) for t in ffn_terms[:3]]
    d_middle, ffn_parts = lax.optimization_barrier((d_middle, ffn_parts))
    grad_gate, grad_up, grad_down = sum_all(ffn_parts, shards, replicas)
    grad_inputs, attn_terms = backward_attn(kept, d_middle, mats)
    g_query_w, g_key_w, g_value_w, g_output_w, g_input, g_query, g_key, g_attend = attn_terms
    g_ffn, g_post = ffn_terms[3:]

    gain_terms = (g_input, g_attend, g_ffn, g_post, g_query, g_key)
    small = jnp.concatenate([g.reshape(shards, -1) for g in gain_terms], axis=1)
    count = small.shape[1]
    rows = -(-count // (2 * width * 64)) * 64
    small = jnp.pad(small, ((0, 0), (0, rows * 2 * width - count)))
    small = small.reshape(shards, rows, 2 * width)
    key_value = jnp.concatenate([g_key_w, g_value_w], axis=1)
    own = key_value.shape[0] // shards
    key_value = jnp.concatenate([key_value.reshape(shards, own, 2 * width), small], axis=1)
    key_value = key_value.reshape(shards * (own + rows), 2 * width)
    attn_parts = [t.astype(jnp.bfloat16) for t in (g_query_w, g_output_w, key_value)]
    grad_query, grad_output, key_value = sum_all(attn_parts, shards, replicas)
    key_value = key_value.astype(jnp.float32)
    small = key_value[own:].reshape(-1)
    grad_gains = []
    place = 0
    for gain in owned_gains:
        grad_gains.append(small[place : place + gain.shape[0]])
        place += gain.shape[0]
    return (
        result.astype(jnp.bfloat16)[None],
        grad_inputs.astype(jnp.bfloat16)[None],
        grad_query.astype(jnp.float32),
        key_value[:own, :width],
        key_value[:own, width:],
        grad_output.astype(jnp.float32),
        grad_gate.astype(jnp.float32),
        grad_up.astype(jnp.float32),
        grad_down.astype(jnp.float32),
        grad_gains[0],
        grad_gains[4],
        grad_gains[5],
        grad_gains[1],
        grad_gains[2],
        grad_gains[3],
    )


def solution(mesh):
    in_specs = (
        P(("rep", "shard"), None, None),
        P(("rep", "shard"), None),
        P("shard", None),
        P("shard", None),
        P("shard", None),
        P("shard", None),
        P("shard", None),
        P("shard", None),
        P("shard", None),
        P("shard"),
        P("shard"),
        P("shard"),
        P("shard"),
        P("shard"),
        P("shard"),
        P(("rep", "shard"), None, None),
    )
    out_specs = (
        P(("rep", "shard"), None, None),
        P(("rep", "shard"), None, None),
        P("shard", None),
        P("shard", None),
        P("shard", None),
        P("shard", None),
        P("shard", None),
        P("shard", None),
        P("shard", None),
        P("shard"),
        P("shard"),
        P("shard"),
        P("shard"),
        P("shard"),
        P("shard"),
    )
    return jax.shard_map(
        functools.partial(per_device, mesh.shape["shard"], mesh.shape["rep"]),
        mesh=mesh, in_specs=in_specs, out_specs=out_specs, check_vma=False
    )
```

```python
import functools

import jax
import jax.numpy as jnp
from jax import lax
from jax.sharding import PartitionSpec as P

EPS = 1e-06
THETA = 1000000.0
BLOCK = 256
DOC_MOST = 512
TIED = (2,)


def norm_rows(values, gain):
    return values * lax.rsqrt(jnp.mean(values * values, axis=-1, keepdims=True) + EPS) * gain


def rotary(values, cosine, sine_part):
    halfway = values.shape[-1] // 2
    front = values[..., :halfway]
    behind = values[..., halfway:]
    return jnp.concatenate(
        [front * cosine - behind * sine_part, behind * cosine + front * sine_part], axis=-1
    )


def rotary_tables(segment, width):
    length = segment.shape[0]
    indices = jnp.arange(length, dtype=jnp.int32)
    change = jnp.concatenate([jnp.ones((1,), dtype=bool), segment[1:] != segment[:-1]])
    starts = lax.cummax(jnp.where(change, indices, 0), axis=0)
    position = (indices - starts).astype(jnp.float32)
    halfway = width // 2
    frequency = THETA ** (-(2.0 * jnp.arange(halfway, dtype=jnp.float32)) / (2.0 * halfway))
    turned = position[:, None] * frequency[None, :]
    return (jnp.cos(turned), jnp.sin(turned))


def glu_part(gate_out, upward):
    return jax.nn.gelu(gate_out, approximate=True) * upward


def block_mask(segment, start, low, high):
    rows_idx = jnp.arange(start, high, dtype=jnp.int32)
    cols_idx = jnp.arange(low, high, dtype=jnp.int32)
    same_doc = segment[start:high][:, None] == segment[low:high][None, :]
    return same_doc & (rows_idx[:, None] >= cols_idx[None, :])


def forward(inputs, segment, mats):
    (
        w_query,
        w_key,
        w_value,
        w_output,
        w_gate,
        w_up,
        w_down,
        gain_input,
        gain_query,
        gain_key,
        gain_attend,
        gain_ffn,
        gain_post,
    ) = mats
    length = inputs.shape[0]
    width = w_key.shape[1]
    heads = w_query.shape[1] // width
    block = min(BLOCK, length)
    cosine, sine_part = rotary_tables(segment, width)
    normed = norm_rows(inputs, gain_input.astype(jnp.float32)).astype(jnp.bfloat16)
    query_raw = jnp.dot(normed, w_query, preferred_element_type=jnp.float32).reshape(
        length, heads, width
    )
    key_raw = jnp.dot(normed, w_key, preferred_element_type=jnp.float32)
    values = jnp.dot(normed, w_value, preferred_element_type=jnp.float32).astype(jnp.bfloat16)
    queries = (
        rotary(
            norm_rows(query_raw, gain_query.astype(jnp.float32)),
            cosine[:, None, :],
            sine_part[:, None, :],
        )
        * width ** (-0.5)
    ).astype(jnp.bfloat16)
    keys_rot = rotary(norm_rows(key_raw, gain_key.astype(jnp.float32)), cosine, sine_part).astype(
        jnp.bfloat16
    )
    pieces = []
    kept_probs = []
    for start in range(0, length, block):
        low = max(0, start - DOC_MOST)
        high = start + block
        scores = jnp.einsum(
            "lhd,md->hlm",
            queries[start:high],
            keys_rot[low:high],
            preferred_element_type=jnp.float32,
        )
        allowed = block_mask(segment, start, low, high)
        scores = jnp.where(allowed[None], scores, -1e30)
        largest = jnp.max(scores, axis=-1, keepdims=True)
        expd = jnp.exp(scores - largest)
        totals = jnp.sum(expd, axis=-1, keepdims=True)
        probabilities = (expd / totals).astype(jnp.bfloat16)
        kept_probs.append(probabilities)
        pieces.append(
            jnp.einsum(
                "hlm,md->lhd", probabilities, values[low:high], preferred_element_type=jnp.float32
            )
        )
    attended = jnp.concatenate(pieces, axis=0).astype(jnp.bfloat16).reshape(length, heads * width)
    branch = jnp.dot(attended, w_output, preferred_element_type=jnp.float32)
    middle = inputs + norm_rows(branch, gain_attend.astype(jnp.float32))
    normed_two = norm_rows(middle, gain_ffn.astype(jnp.float32)).astype(jnp.bfloat16)
    gate_out = jnp.dot(normed_two, w_gate, preferred_element_type=jnp.float32)
    upward = jnp.dot(normed_two, w_up, preferred_element_type=jnp.float32)
    hidden = glu_part(gate_out, upward).astype(jnp.bfloat16)
    branch_two = jnp.dot(hidden, w_down, preferred_element_type=jnp.float32)
    result = middle + norm_rows(branch_two, gain_post.astype(jnp.float32))
    kept = (
        inputs,
        segment,
        cosine,
        sine_part,
        normed,
        query_raw,
        key_raw,
        values,
        queries,
        keys_rot,
        kept_probs,
        attended,
        branch,
        middle,
        normed_two,
        gate_out,
        upward,
        hidden,
        branch_two,
    )
    return (result, kept)


def backward_ffn(kept, incoming, mats):
    (
        w_query,
        w_key,
        w_value,
        w_output,
        w_gate,
        w_up,
        w_down,
        gain_input,
        gain_query,
        gain_key,
        gain_attend,
        gain_ffn,
        gain_post,
    ) = mats
    (
        inputs,
        segment,
        cosine,
        sine_part,
        normed,
        query_raw,
        key_raw,
        values,
        queries,
        keys_rot,
        kept_probs,
        attended,
        branch,
        middle,
        normed_two,
        gate_out,
        upward,
        hidden,
        branch_two,
    ) = kept
    grad_out = incoming.astype(jnp.float32)
    unused, pull_post = jax.vjp(norm_rows, branch_two, gain_post.astype(jnp.float32))
    d_branch_two, g_post = pull_post(grad_out)
    d_branch_two = d_branch_two.astype(jnp.bfloat16)
    gw_down = jnp.einsum("lf,ld->fd", hidden, d_branch_two, preferred_element_type=jnp.float32)
    d_hidden = jnp.einsum("ld,fd->lf", d_branch_two, w_down, preferred_element_type=jnp.float32)
    unused, pull_glu = jax.vjp(glu_part, gate_out, upward)
    d_gate, d_up = pull_glu(d_hidden)
    d_gate = d_gate.astype(jnp.bfloat16)
    d_up = d_up.astype(jnp.bfloat16)
    gw_gate = jnp.einsum("ld,lf->df", normed_two, d_gate, preferred_element_type=jnp.float32)
    gw_up = jnp.einsum("ld,lf->df", normed_two, d_up, preferred_element_type=jnp.float32)
    d_normed_two = jnp.einsum(
        "lf,df->ld", d_gate, w_gate, preferred_element_type=jnp.float32
    ) + jnp.einsum("lf,df->ld", d_up, w_up, preferred_element_type=jnp.float32)
    unused, pull_ffn = jax.vjp(norm_rows, middle, gain_ffn.astype(jnp.float32))
    d_mid_part, g_ffn = pull_ffn(d_normed_two)
    d_middle = grad_out + d_mid_part
    return (d_middle, (gw_gate, gw_up, gw_down, g_ffn, g_post))


def backward_attn(kept, d_middle, mats, begin):
    (
        w_query,
        w_key,
        w_value,
        w_output,
        w_gate,
        w_up,
        w_down,
        gain_input,
        gain_query,
        gain_key,
        gain_attend,
        gain_ffn,
        gain_post,
    ) = mats
    (
        inputs,
        segment,
        cosine,
        sine_part,
        normed,
        query_raw,
        key_raw,
        values,
        queries,
        keys_rot,
        kept_probs,
        attended,
        branch,
        middle,
        normed_two,
        gate_out,
        upward,
        hidden,
        branch_two,
    ) = kept
    length = inputs.shape[0]
    width = w_key.shape[1]
    heads = w_query.shape[1] // width
    block = min(BLOCK, length)
    unused, pull_attend = jax.vjp(norm_rows, branch, gain_attend.astype(jnp.float32))
    d_branch, g_attend = pull_attend(d_middle)
    d_branch = d_branch.astype(jnp.bfloat16)
    gw_output = jnp.einsum("la,ld->ad", attended, d_branch, preferred_element_type=jnp.float32)
    d_attended = jnp.einsum("ld,ad->la", d_branch, w_output, preferred_element_type=jnp.float32)
    d_attended = d_attended.astype(jnp.bfloat16).reshape(length, heads, width)
    d_attended, gw_output = lax.optimization_barrier(
        (d_attended, gw_output.astype(jnp.bfloat16))
    )
    summing = begin(gw_output)
    attended_heads = attended.reshape(length, heads, width)
    delta = jnp.sum(
        d_attended.astype(jnp.float32) * attended_heads.astype(jnp.float32), axis=-1
    ).T
    d_keys = [0.0] * (length // block)
    d_values = [0.0] * (length // block)
    d_query_parts = []
    for number, start in enumerate(range(0, length, block)):
        low = max(0, start - DOC_MOST)
        high = start + block
        rows_q = queries[start:high]
        if number in TIED:
            d_attended, d_query_parts, d_keys, d_values = summing.tie(
                (d_attended, d_query_parts, d_keys, d_values)
            )
        rows_d = d_attended[start:high]
        probabilities = kept_probs[number]
        value_term = jnp.einsum(
            "hlm,lhd->md", probabilities, rows_d, preferred_element_type=jnp.float32
        )
        d_probs = jnp.einsum(
            "lhd,md->hlm", rows_d, values[low:high], preferred_element_type=jnp.float32
        )
        d_scores = probabilities.astype(jnp.float32) * (d_probs - delta[:, start:high, None])
        d_scores = d_scores.astype(jnp.bfloat16)
        d_query_parts.append(
            jnp.einsum(
                "hlm,md->lhd", d_scores, keys_rot[low:high], preferred_element_type=jnp.float32
            )
        )
        key_term = jnp.einsum("hlm,lhd->md", d_scores, rows_q, preferred_element_type=jnp.float32)
        for part in range(low // block, high // block):
            rows = slice(part * block - low, part * block - low + block)
            d_keys[part] = d_keys[part] + key_term[rows]
            d_values[part] = d_values[part] + value_term[rows]
    d_query_parts, d_keys, d_values = summing.tie((d_query_parts, d_keys, d_values))
    d_queries = jnp.concatenate(d_query_parts, axis=0)
    d_keys = jnp.concatenate(d_keys, axis=0)
    d_values = jnp.concatenate(d_values, axis=0)

    def query_map(raw_query, gain_value):
        return rotary(
            norm_rows(raw_query, gain_value), cosine[:, None, :], sine_part[:, None, :]
        ) * width ** (-0.5)

    def key_map(raw_key, gain_value):
        return rotary(norm_rows(raw_key, gain_value), cosine, sine_part)

    unused, pull_query = jax.vjp(query_map, query_raw, gain_query.astype(jnp.float32))
    d_query_raw, g_query = pull_query(d_queries)
    d_query_raw = d_query_raw.astype(jnp.bfloat16).reshape(length, heads * width)
    unused, pull_key = jax.vjp(key_map, key_raw, gain_key.astype(jnp.float32))
    d_key_raw, g_key = pull_key(d_keys)
    d_key_raw = d_key_raw.astype(jnp.bfloat16)
    d_values = d_values.astype(jnp.bfloat16)
    d_query_raw, d_key_raw, d_values = summing.tie((d_query_raw, d_key_raw, d_values))
    gw_query = jnp.einsum("ld,lq->dq", normed, d_query_raw, preferred_element_type=jnp.float32)
    gw_key = jnp.einsum("ld,lq->dq", normed, d_key_raw, preferred_element_type=jnp.float32)
    gw_value = jnp.einsum("ld,lq->dq", normed, d_values, preferred_element_type=jnp.float32)
    d_normed = (
        jnp.einsum("lq,dq->ld", d_query_raw, w_query, preferred_element_type=jnp.float32)
        + jnp.einsum("lq,dq->ld", d_key_raw, w_key, preferred_element_type=jnp.float32)
        + jnp.einsum("lq,dq->ld", d_values, w_value, preferred_element_type=jnp.float32)
    )
    unused, pull_input = jax.vjp(norm_rows, inputs, gain_input.astype(jnp.float32))
    d_in_part, g_input = pull_input(d_normed)
    grad_inputs = d_middle + d_in_part
    return (grad_inputs, summing, (gw_query, gw_key, gw_value, g_input, g_query, g_key, g_attend))


def flip_bit(size, bit):
    return [(i, i ^ (1 << bit)) for i in range(size)]


def half_axis(shape):
    if shape[1] % 256 == 0:
        return 1
    if shape[0] % 2 == 0:
        return 0
    return 1


def halves(x, axis):
    half = x.shape[axis] // 2
    return (
        lax.slice_in_dim(x, 0, half, axis=axis),
        lax.slice_in_dim(x, half, 2 * half, axis=axis),
    )


def exchange_sum(x, name, size, bit, axis):
    upper = ((lax.axis_index(name) >> bit) & 1) == 1
    low, high = halves(x, axis)
    away = lax.ppermute(jnp.where(upper, low, high), name, flip_bit(size, bit))
    kept = jnp.where(upper, high, low)
    return (kept.astype(jnp.float32) + away.astype(jnp.float32)).astype(x.dtype)


def exchange_join(x, name, size, bit, axis):
    upper = ((lax.axis_index(name) >> bit) & 1) == 1
    other = lax.ppermute(x, name, flip_bit(size, bit))
    return jnp.concatenate(
        [jnp.where(upper, other, x), jnp.where(upper, x, other)], axis=axis
    )


def bit_count(size):
    count = size.bit_length() - 1
    assert size == 1 << count
    return count


def gather_rows(x, size):
    for bit in range(bit_count(size)):
        x = exchange_join(x, "shard", size, bit, 0)
    return x


def sum_stages(parts, shards, replicas):
    parts = list(parts)
    for bit in reversed(range(bit_count(shards))):
        parts = [exchange_sum(x, "shard", shards, bit, 0) for x in parts]
    parts = yield parts
    count = bit_count(replicas)
    orders = []
    for number in range(len(parts)):
        base = list(range(count - 1))
        turn = number % max(len(base), 1)
        orders.append(base[turn:] + base[:turn] + [count - 1])
    done = [[] for _ in parts]
    for step in range(count):
        for number in range(len(parts)):
            axis = half_axis(parts[number].shape)
            done[number].append((orders[number][step], axis))
            parts[number] = exchange_sum(
                parts[number], "rep", replicas, orders[number][step], axis
            )
        parts = yield parts
    for step in reversed(range(count)):
        for number in range(len(parts)):
            bit, axis = done[number][step]
            parts[number] = exchange_join(parts[number], "rep", replicas, bit, axis)
        parts = yield parts


class Summing:
    def __init__(self, parts, shards, replicas):
        self.stages = sum_stages(parts, shards, replicas)
        self.left = 1 + 2 * bit_count(replicas)
        self.parts = next(self.stages)
        self.left -= 1

    def advance(self):
        if self.left:
            self.parts = list(self.stages.send(self.parts))
            self.left -= 1

    def tie(self, value):
        value, self.parts = lax.optimization_barrier((value, self.parts))
        self.parts = list(self.parts)
        self.advance()
        return value


def per_device(
    shards,
    replicas,
    tokens,
    segments,
    w_query,
    w_key,
    w_value,
    w_output,
    w_gate,
    w_up,
    w_down,
    gain_input,
    gain_query,
    gain_key,
    gain_attend,
    gain_ffn,
    gain_post,
    cotangent,
):
    queries_wide = w_query.shape[1]
    width = w_key.shape[1]
    w_all = gather_rows(jnp.concatenate([w_query, w_key, w_value], axis=1), shards)
    owned_gains = (gain_input, gain_attend, gain_ffn, gain_post, gain_query, gain_key)
    packed = gather_rows(jnp.concatenate(owned_gains)[None], shards)
    gains = []
    place = 0
    for gain in owned_gains:
        gains.append(packed[:, place : place + gain.shape[0]].reshape(-1))
        place += gain.shape[0]
    mats = (
        w_all[:, :queries_wide],
        w_all[:, queries_wide : queries_wide + width],
        w_all[:, queries_wide + width :],
        lax.all_gather(w_output, "shard", axis=0, tiled=True),
        lax.all_gather(w_gate, "shard", axis=0, tiled=True),
        lax.all_gather(w_up, "shard", axis=0, tiled=True),
        lax.all_gather(w_down, "shard", axis=0, tiled=True),
        gains[0],
        gains[4],
        gains[5],
        gains[1],
        gains[2],
        gains[3],
    )
    result, kept = forward(tokens[0].astype(jnp.float32), segments[0], mats)
    d_middle, ffn_terms = backward_ffn(kept, cotangent[0], mats)
    ffn_parts = [t.astype(jnp.bfloat16) for t in ffn_terms[:3]]
    d_middle, ffn_parts = lax.optimization_barrier((d_middle, ffn_parts))

    def begin(grad_output):
        rows_all = jnp.concatenate(
            [x.reshape(shards, -1, x.shape[1]) for x in (ffn_parts[2], grad_output)], axis=1
        ).reshape(-1, grad_output.shape[1])
        return Summing(ffn_parts[:2] + [rows_all], shards, replicas)

    ffn_parts = list(ffn_parts)
    grad_inputs, early, attn_terms = backward_attn(kept, d_middle, mats, begin)
    g_query_w, g_key_w, g_value_w, g_input, g_query, g_key, g_attend = attn_terms
    g_ffn, g_post = ffn_terms[3:]

    gain_terms = (g_input, g_attend, g_ffn, g_post, g_query, g_key)
    small = jnp.concatenate([g.reshape(shards, -1) for g in gain_terms], axis=1)
    count = small.shape[1]
    rows = -(-count // (2 * width * 16)) * 16
    small = jnp.pad(small, ((0, 0), (0, rows * 2 * width - count)))
    small = small.reshape(shards, rows, 2 * width)
    key_value = jnp.concatenate([g_key_w, g_value_w], axis=1)
    own = key_value.shape[0] // shards
    key_value = jnp.concatenate([key_value.reshape(shards, own, 2 * width), small], axis=1)
    key_value = key_value.reshape(shards * (own + rows), 2 * width)
    wide = g_query_w.reshape(shards, own, queries_wide)
    wide = jnp.pad(wide, ((0, 0), (0, rows), (0, 0)))
    wide = wide.reshape(shards * (own + rows), queries_wide)
    attn_parts = [jnp.concatenate([wide, key_value], axis=1).astype(jnp.bfloat16)]
    attn_parts = early.tie(attn_parts)
    late = Summing(attn_parts, shards, replicas)
    while late.left:
        if early.left:
            late.parts = list(early.tie(late.parts))
        late.advance()
    while early.left:
        early.advance()
    grad_gate, grad_up, rows_all = early.parts
    down_rows = ffn_parts[2].shape[0] // shards
    grad_down, grad_output = rows_all[:down_rows], rows_all[down_rows:]
    late_sum = late.parts[0]
    grad_query = late_sum[:own, :queries_wide]
    key_value = late_sum[:, queries_wide:]
    key_value = key_value.astype(jnp.float32)
    small = key_value[own:].reshape(-1)
    grad_gains = []
    place = 0
    for gain in owned_gains:
        grad_gains.append(small[place : place + gain.shape[0]])
        place += gain.shape[0]
    return (
        result.astype(jnp.bfloat16)[None],
        grad_inputs.astype(jnp.bfloat16)[None],
        grad_query.astype(jnp.float32),
        key_value[:own, :width],
        key_value[:own, width:],
        grad_output.astype(jnp.float32),
        grad_gate.astype(jnp.float32),
        grad_up.astype(jnp.float32),
        grad_down.astype(jnp.float32),
        grad_gains[0],
        grad_gains[4],
        grad_gains[5],
        grad_gains[1],
        grad_gains[2],
        grad_gains[3],
    )


def solution(mesh):
    in_specs = (
        P(("rep", "shard"), None, None),
        P(("rep", "shard"), None),
        P("shard", None),
        P("shard", None),
        P("shard", None),
        P("shard", None),
        P("shard", None),
        P("shard", None),
        P("shard", None),
        P("shard"),
        P("shard"),
        P("shard"),
        P("shard"),
        P("shard"),
        P("shard"),
        P(("rep", "shard"), None, None),
    )
    out_specs = (
        P(("rep", "shard"), None, None),
        P(("rep", "shard"), None, None),
        P("shard", None),
        P("shard", None),
        P("shard", None),
        P("shard", None),
        P("shard", None),
        P("shard", None),
        P("shard", None),
        P("shard"),
        P("shard"),
        P("shard"),
        P("shard"),
        P("shard"),
        P("shard"),
    )
    return jax.shard_map(
        functools.partial(per_device, mesh.shape["shard"], mesh.shape["rep"]),
        mesh=mesh, in_specs=in_specs, out_specs=out_specs, check_vma=False
    )
```
